512 devices in a mesh: tm: 16 (over y, core), tile: 32 (over x, z).
Axes of the slice: x: 4, y: 8, z: 8, core: 2. Of those that a mesh axis runs over, the one named last changes fastest.
Arguments:
- latents: bfloat16 [32, 64, 2560], P('tm', 'tile'), may hold values from -16 to 16
- frame_slot: int32 [32], replicated, may hold values from 0 to 31, as said below
- lengths: int32 [4], replicated, may hold values from 1 to 16, 32 in all
- w_in: bfloat16 [16, 27, 192], replicated, may hold values from -0.3125 to 0.3125
- bias_in: float32 [192], replicated, may hold values from -3 to 3
- norm_gain: float32 [192], replicated, may hold values from 0.1 to 1.9
- w_mid: bfloat16 [192, 27, 192], replicated, may hold values from -0.078125 to 0.078125
- bias_mid: float32 [192], replicated, may hold values from -3 to 3
Outputs:
- decoded: bfloat16 [32, 64, 160, 192], P('tm', 'tile')
The draws below stay inside these ranges and needn't reach their ends.
Inputs may be any that keep to these rules, and one draw needn't show every extreme that they name: `frame_slot`: each time position appears once. The lengths sum to 32.
All inputs are finite; a program needn't handle non-finite values.
Results may differ from the reference program's by a relative error of at most 0.013.
Values may be sent and summed in bfloat16 or wider, within the bound.
No kernel may reach another device: no remote copies, remote signals or barrier semaphores. Data moves between devices by JAX's collectives and lax.ppermute only.
A program may use at most 64 MiB of HBM per device.

```python
import math
import jax
import jax.numpy as jnp
import numpy as np
from jax import lax

ZC = 16
C = 192
GROUPS = 32
ROLLS = 4
TH = 2
W = 160
FRAMES = 32
H = 64
MOST = 16


def draw_latents(key, part):
    key = jax.random.fold_in(key, 7)
    key_base = jax.random.fold_in(key, 0)
    key_cols = jax.random.fold_in(key, 1)
    key_sign = jax.random.fold_in(key, 3)
    key_rough = jax.random.fold_in(key, 4)
    row_scale = 0.1 * 10.0 ** (jnp.arange(H, dtype=jnp.float32) / (H - 1))
    col_scale = jnp.exp(jax.random.uniform(key_cols, (W,), jnp.float32, -0.6, 0.6))
    parity = (jnp.arange(H, dtype=jnp.int32) // TH % 2).astype(jnp.float32) * 2.0 - 1.0
    frame_sign = jnp.where(jax.random.bernoulli(key_sign, 0.5, (FRAMES,)), 1.0, -1.0).astype(jnp.float32)
    rough = jax.random.uniform(key_rough, (FRAMES, H), jnp.float32, -0.5, 0.5)
    row_factor = jnp.exp(1.1 * frame_sign[:, None] * parity[None, :] + rough)
    base = jnp.clip(jax.random.normal(key_base, (FRAMES, H, W, ZC), jnp.float32), -4.0, 4.0)
    values = 0.6 * base * row_scale[None, :, None, None] * col_scale[None, None, :, None]
    values = values * row_factor[:, :, None, None]
    values = jnp.clip(values, -15.5, 15.5)
    return values.reshape(FRAMES, H, W * ZC).astype(jnp.bfloat16)


def draw_frame_slot(key, part):
    key = jax.random.fold_in(key, 11)
    shuffled = jax.random.permutation(key, FRAMES).astype(jnp.int32)
    positions = jnp.arange(FRAMES, dtype=jnp.int32)
    where_zero = jnp.sum(jnp.where(shuffled == 0, positions, 0)).astype(jnp.int32)
    target = FRAMES // 2
    moved = shuffled[target]
    result = jnp.where(positions == where_zero, moved, shuffled)
    result = jnp.where(positions == target, jnp.int32(0), result)
    return result.astype(jnp.int32)


def split_up(amount, total, reach, lean):
    portions = [(1 << 20) // math.isqrt(grade ** lean) + 1 for grade in range(2, amount + 1)]
    rest, holding = total - reach - (amount - 1), [1] * (amount - 1)
    while rest > 0:
        free = [i for i in range(amount - 1) if holding[i] < reach]
        whole, left = sum([portions[i] for i in free]), rest
        for i in free:
            more = min(reach - holding[i], max(1, left * portions[i] // whole), rest)
            holding[i] = holding[i] + more
            rest = rest - more
    return np.array([reach] + holding)


def ragged(key, count, total, most, slope):
    if count == 2:
        one = jax.random.randint(key, (), max(1, total - most), min(most, total - 1) + 1)
        return jnp.stack([one, total - one])
    tallies = jnp.asarray(split_up(count, total, most, slope), jnp.int32)
    pairs = (count - 1) // 2
    giver, receiver = tallies[1:1 + 2 * pairs:2], tallies[2:2 + 2 * pairs:2]
    slack = jnp.minimum(giver - 1, most - receiver)
    shifted = jax.random.randint(jax.random.fold_in(key, 1), (pairs,), 0, 1 << 20) % (slack + 1)
    tallies = tallies.at[1:1 + 2 * pairs:2].set(giver - shifted).at[2:2 + 2 * pairs:2].set(receiver + shifted)
    return tallies[jax.random.permutation(jax.random.fold_in(key, 2), count)]


def noise(key, dims, scale, most, kind=jnp.bfloat16):
    array = jax.random.normal(key, dims, jnp.float32) * scale
    return jnp.minimum(jnp.maximum(array, -most), most).astype(kind)


def setup_inputs(seed: int = 0) -> dict:
    streams_of = jax.random.split(jax.random.key(seed), 9)
    latents = draw_latents(jax.random.fold_in(streams_of[8], 71), 0)
    frame_slot = draw_frame_slot(jax.random.fold_in(streams_of[8], 71), 0)
    lengths = ragged(streams_of[2], ROLLS, FRAMES, MOST, 2).astype(jnp.int32)
    w_in = noise(streams_of[3], (ZC, 27, C), (27 * ZC) ** -0.5, 0.3125)
    bias_in = noise(streams_of[4], (C,), 0.5, 3.0, jnp.float32)
    norm_gain = jnp.clip(1.0 + 0.18 * jax.random.normal(streams_of[5], (C,), jnp.float32), 0.1, 1.9)
    w_mid = noise(streams_of[6], (C, 27, C), (27 * C) ** -0.5, 0.078125)
    bias_mid = noise(streams_of[7], (C,), 0.5, 3.0, jnp.float32)
    return dict(latents=latents, frame_slot=frame_slot, lengths=lengths, w_in=w_in, bias_in=bias_in, norm_gain=norm_gain, w_mid=w_mid, bias_mid=bias_mid)


def rollout_starts(lengths):
    rollout_ends = jnp.cumsum(lengths).astype(jnp.int32)
    frame_index = jnp.arange(FRAMES, dtype=jnp.int32)
    closed = rollout_ends[None, :] <= frame_index[:, None]
    return lax.optimization_barrier(jnp.sum(jnp.where(closed, lengths[None, :], 0), axis=1)).astype(jnp.int32)

def causal_conv(source, weight, bias, rollout_begin):
    padded = jnp.pad(source, ((2, 0), (1, 1), (1, 1), (0, 0)))
    weight_f = weight.astype(jnp.float32)

    def one_frame(frame_index):
        taps_list = []
        for k in range(3):
            usable = (frame_index - 2 + k >= rollout_begin[frame_index]).astype(source.dtype)
            plane = lax.dynamic_slice_in_dim(padded, frame_index + k, 1, 0)[0] * usable
            for dy in range(3):
                for dx in range(3):
                    taps_list.append(plane[dy:dy + H, dx:dx + W])
        patches = jnp.stack(taps_list, axis=2).astype(jnp.float32)
        return jnp.einsum('hwkn,nko->hwo', patches, weight_f)
    return lax.map(one_frame, jnp.arange(FRAMES, dtype=jnp.int32)) + bias

def reference(latents, frame_slot, lengths, w_in, bias_in, norm_gain, w_mid, bias_mid):
    ordered = jnp.zeros_like(latents).at[frame_slot].set(latents)
    ordered = ordered.reshape(FRAMES, H, W, ZC)
    rollout_begin = rollout_starts(lengths)
    hidden = causal_conv(ordered, w_in, bias_in, rollout_begin).astype(jnp.bfloat16)
    hidden_f = hidden.astype(jnp.float32).reshape(FRAMES, H * W, GROUPS, C // GROUPS)
    entries = H * W * (C // GROUPS)
    average = lax.optimization_barrier(jnp.sum(hidden_f, axis=(1, 3))) / entries
    mean_square = lax.optimization_barrier(jnp.sum(hidden_f * hidden_f, axis=(1, 3))) / entries
    variance = mean_square - average * average
    normed = (hidden_f - average[:, None, :, None]) * lax.rsqrt(variance + 1e-06)[:, None, :, None]
    activated = jax.nn.silu(normed.reshape(FRAMES, H, W, C) * norm_gain).astype(jnp.bfloat16)
    branch = causal_conv(activated, w_mid, bias_mid, rollout_begin)
    return (hidden.astype(jnp.float32) + branch).astype(jnp.bfloat16)
```

```python
import jax
import jax.numpy as jnp
from jax import lax
from jax.sharding import PartitionSpec as P

GROUPS = 32


def begins(lengths, frame_index):
    ends = jnp.cumsum(lengths)
    closed = ends[None, :] <= frame_index[:, None]
    return jnp.sum(jnp.where(closed, lengths[None, :], 0), axis=1)


def convolve(extended, usable, weight, frames, rows, width):
    total = None
    padded = jnp.pad(extended, ((0, 0), (0, 0), (1, 1), (0, 0)))
    for k in range(3):
        planes = jnp.stack([padded[i + k] * usable[i, k] for i in range(frames)], axis=0)
        taps = []
        for dy in range(3):
            for dx in range(3):
                taps.append(planes[:, dy : dy + rows, dx : dx + width])
        patches = jnp.stack(taps, axis=3).reshape(frames * rows * width, 9, -1)
        term = jnp.einsum(
            "ckn,nko->co",
            patches,
            weight[:, 9 * k : 9 * k + 9, :],
            preferred_element_type=jnp.float32,
        )
        total = term if total is None else total + term
    return total


def body(latents, frame_slot, lengths, w_in, bias_in, norm_gain, w_mid, bias_mid):
    rows = latents.shape[1]
    zc = w_in.shape[0]
    channels = w_in.shape[2]
    width = latents.shape[2] // zc
    per_group = channels // GROUPS
    tiles = lax.axis_size("tile")
    tile = lax.axis_index("tile")
    first = 2 * lax.axis_index("tm")
    own = first + jnp.arange(-4, 2, dtype=jnp.int32)
    onehot = (frame_slot[None, :] == own[:, None]).astype(jnp.bfloat16)
    gathered = lax.all_gather(latents, "tm", axis=0, tiled=True)
    picked = jnp.dot(
        onehot, gathered.reshape(gathered.shape[0], -1), preferred_element_type=jnp.float32
    )
    picked = picked.astype(jnp.bfloat16).reshape(6, rows, -1)
    above = lax.ppermute(picked, "tile", [(i, i + 1) for i in range(tiles - 1)])
    below = lax.ppermute(picked, "tile", [(i + 1, i) for i in range(tiles - 1)])
    ext = jnp.concatenate([above, picked, below], axis=1).reshape(6, 3 * rows, width, zc)

    frames = first + jnp.arange(-2, 2, dtype=jnp.int32)
    begin = begins(lengths, frames)
    sources = frames[:, None] - 2 + jnp.arange(3, dtype=jnp.int32)[None, :]
    usable = (sources >= begin[:, None]).astype(jnp.bfloat16)

    hidden = (convolve(ext, usable, w_in, 4, 4, width) + bias_in).astype(jnp.bfloat16)
    hidden = hidden.reshape(4, 4, width, channels)
    hidden_f = hidden.astype(jnp.float32)
    mine = hidden_f[:, 1:3]
    sums = jnp.stack([jnp.sum(mine, axis=(1, 2)), jnp.sum(mine * mine, axis=(1, 2))], axis=1)
    sums = jnp.sum(sums.reshape(4, 2, GROUPS, per_group), axis=3)
    block = jnp.broadcast_to(sums.reshape(1, 2, 128), (tiles, 2, 128))
    sums = jnp.sum(lax.all_to_all(block, "tile", 0, 0), axis=0).reshape(4, 2, GROUPS)
    entries = rows * tiles * width * per_group
    average = sums[:, 0] / entries
    variance = sums[:, 1] / entries - average * average
    scale = lax.rsqrt(variance + 1e-06)
    average = jnp.repeat(average, per_group, axis=1)[:, None, None, :]
    scale = jnp.repeat(scale, per_group, axis=1)[:, None, None, :]
    activated = jax.nn.silu((hidden_f - average) * scale * norm_gain).astype(jnp.bfloat16)
    grid_rows = rows * tile - 1 + jnp.arange(4)
    inside = (grid_rows >= 0) & (grid_rows < rows * tiles)
    activated = jnp.where(inside[None, :, None, None], activated, jnp.bfloat16(0))
    branch = convolve(activated, usable[2:], w_mid, 2, 2, width)
    decoded = mine[2:].reshape(-1, channels) + branch + bias_mid
    return decoded.astype(jnp.bfloat16).reshape(2, rows, width, channels)


def solution(mesh):
    return jax.shard_map(
        body,
        mesh=mesh,
        in_specs=(P("tm", "tile", None), P(), P(), P(), P(), P(), P(), P()),
        out_specs=P("tm", "tile", None, None),
        check_vma=False,
    )
```

```python
import jax
import jax.numpy as jnp
from jax import lax
from jax.experimental import pallas as pl
from jax.experimental.pallas import tpu as pltpu
from jax.sharding import PartitionSpec as P

GROUPS = 32
LANES = 256
VMEM = pl.BlockSpec(memory_space=pltpu.VMEM)
SMEM = pl.BlockSpec(memory_space=pltpu.SMEM)
F32 = jnp.float32
BF16 = jnp.bfloat16
PARAMS = pltpu.CompilerParams(vmem_limit_bytes=48 * 1024 * 1024)


def usable(lengths_ref, frame, k):
    begin = jnp.int32(0)
    end = jnp.int32(0)
    for r in range(lengths_ref.shape[0]):
        end = end + lengths_ref[r]
        begin = jnp.where(end <= frame, end, begin)
    return (frame - 2 + k) >= begin


def roll_both(v):
    return pltpu.roll(v, 1, 1), pltpu.roll(v, LANES - 1, 1)


def pick_kernel(slot_ref, gathered_ref, picked_ref):
    base = 2 * lax.axis_index("tm") - 4
    picked_ref[...] = jnp.zeros_like(picked_ref)

    @pl.loop(0, slot_ref.shape[0])
    def _(p):
        j = slot_ref[p] - base

        @pl.when((j >= 0) & (j < 6))
        def _():
            picked_ref[j] = gathered_ref[p]


def group_mask(channels, frame):
    per_group = channels // GROUPS
    channel = lax.broadcasted_iota(jnp.int32, (channels, 128), 0)
    lane = lax.broadcasted_iota(jnp.int32, (channels, 128), 1)
    low = (lane - GROUPS * frame) * per_group
    return (channel >= low) & (channel < low + per_group) & (lane >= GROUPS * frame) & (lane < GROUPS * frame + GROUPS)


def hidden_kernel(width, lengths_ref, above_ref, picked_ref, below_ref, w_ref, bias_ref, hidden_ref, sums_ref, xs_ref):
    channels = bias_ref.shape[0]
    first = 2 * lax.axis_index("tm")
    for f in range(6):
        for r in range(6):
            ref = (above_ref, picked_ref, below_ref)[r // 2]
            v = ref[f, r % 2]
            left, right = roll_both(v.astype(F32))
            xs_ref[f, r, 0:16] = left.astype(BF16)
            xs_ref[f, r, 16:32] = v
            xs_ref[f, r, 32:48] = right.astype(BF16)
    bias = bias_ref[...]
    inside = lax.broadcasted_iota(jnp.int32, (channels, LANES), 1) < width
    columns = []
    for j in range(4):
        frame = first - 2 + j
        u0 = usable(lengths_ref, frame, 0).astype(F32)
        u1 = usable(lengths_ref, frame, 1).astype(F32)
        s1 = jnp.zeros((channels, LANES), F32)
        s2 = jnp.zeros((channels, LANES), F32)
        for r in range(4):
            acc = [
                jnp.dot(w_ref[k], xs_ref[j + k, r : r + 3].reshape(144, LANES), preferred_element_type=F32)
                for k in range(3)
            ]
            h = (acc[2] + u1 * acc[1] + u0 * acc[0] + bias).astype(BF16)
            hidden_ref[j, r] = h
            if r in (1, 2):
                hf = jnp.where(inside, h.astype(F32), 0.0)
                s1 = s1 + hf
                s2 = s2 + hf * hf
        columns.append(
            (
                jnp.sum(s1[:, :128] + s1[:, 128:], axis=1, keepdims=True),
                jnp.sum(s2[:, :128] + s2[:, 128:], axis=1, keepdims=True),
            )
        )
    d1 = jnp.zeros((channels, 128), F32)
    d2 = jnp.zeros((channels, 128), F32)
    for j in range(4):
        mask = group_mask(channels, j)
        d1 = jnp.where(mask, columns[j][0], d1)
        d2 = jnp.where(mask, columns[j][1], d2)
    s1 = jnp.sum(d1, axis=0, keepdims=True)
    s2 = jnp.sum(d2, axis=0, keepdims=True)
    block = jnp.concatenate([s1, s2], axis=0)
    sums_ref[...] = jnp.broadcast_to(block[None], sums_ref.shape)


def decode_kernel(width, entries, tiles, lengths_ref, sums_ref, hidden_ref, w_ref, gain_ref, bias_ref, out_ref, act_ref):
    channels = bias_ref.shape[0]
    first = 2 * lax.axis_index("tm")
    tile = lax.axis_index("tile")
    total = jnp.sum(sums_ref[...], axis=0)
    average = total[0:1] / entries
    variance = total[1:2] / entries - average * average
    rstd = lax.rsqrt(variance + 1e-06)
    lane = lax.broadcasted_iota(jnp.int32, (channels, LANES), 1)
    half_gain = 0.5 * gain_ref[...]
    for j in range(4):
        mask = group_mask(channels, j)
        mean = jnp.sum(jnp.where(mask, average, 0.0), axis=1, keepdims=True)
        scale = jnp.sum(jnp.where(mask, rstd, 0.0), axis=1, keepdims=True) * half_gain
        for r in range(4):
            limit = jnp.int32(width)
            if r == 0:
                limit = jnp.where(tile > 0, limit, 0)
            if r == 3:
                limit = jnp.where(tile < tiles - 1, limit, 0)
            u = (hidden_ref[j, r].astype(F32) - mean) * scale
            a = jnp.where(lane < limit, u + u * jnp.tanh(u), 0.0)
            left, right = roll_both(a)
            act_ref[j, r, 0] = left.astype(BF16)
            act_ref[j, r, 1] = a.astype(BF16)
            act_ref[j, r, 2] = right.astype(BF16)
    bias = bias_ref[...]
    for i in range(2):
        u0 = usable(lengths_ref, first + i, 0)
        u1 = usable(lengths_ref, first + i, 1)
        for r in range(2):
            acc = []
            for k in range(3):
                total = None
                for dy in range(3):
                    for dx in range(3):
                        term = jnp.dot(w_ref[9 * k + 3 * dy + dx], act_ref[i + k, r + dy, dx], preferred_element_type=F32)
                        total = term if total is None else total + term
                acc.append(total)
            y = acc[2] + jnp.where(u1, acc[1], 0.0) + jnp.where(u0, acc[0], 0.0)
            y = y + bias + hidden_ref[2 + i, r + 1].astype(F32)
            out_ref[i, r] = y.T[:width].astype(BF16)


def body(latents, frame_slot, lengths, w_in, bias_in, norm_gain, w_mid, bias_mid):
    rows = latents.shape[1]
    zc = w_in.shape[0]
    channels = w_in.shape[2]
    width = latents.shape[2] // zc
    tiles = lax.axis_size("tile")
    lt = jnp.swapaxes(latents.reshape(2, rows, width, zc), 2, 3)
    lt = jnp.pad(lt, ((0, 0), (0, 0), (0, 0), (0, LANES - width)))
    gathered = lax.all_gather(lt, "tm", axis=0, tiled=True)
    picked = pl.pallas_call(
        pick_kernel,
        out_shape=jax.ShapeDtypeStruct((6, rows, zc, LANES), BF16),
        in_specs=[SMEM, VMEM],
        out_specs=VMEM,
        compiler_params=PARAMS,
        name="pick",
    )(frame_slot, gathered)
    above = lax.ppermute(picked, "tile", [(i, i + 1) for i in range(tiles - 1)])
    below = lax.ppermute(picked, "tile", [(i + 1, i) for i in range(tiles - 1)])
    w_in_t = jnp.transpose(w_in.reshape(zc, 3, 9, channels), (1, 3, 2, 0)).reshape(3, channels, 9 * zc)
    w_mid_t = jnp.transpose(w_mid, (1, 2, 0))

    def hidden_body(*refs):
        hidden_kernel(width, *refs)

    hidden, sums = pl.pallas_call(
        hidden_body,
        out_shape=[
            jax.ShapeDtypeStruct((4, 4, channels, LANES), BF16),
            jax.ShapeDtypeStruct((tiles, 2, 128), F32),
        ],
        in_specs=[SMEM] + [VMEM] * 5,
        out_specs=[VMEM, VMEM],
        scratch_shapes=[pltpu.VMEM((6, 6, 3 * zc, LANES), BF16)],
        compiler_params=PARAMS,
        name="hidden",
    )(lengths, above, picked, below, w_in_t, bias_in[:, None])
    sums = lax.all_to_all(sums, "tile", 0, 0)
    entries = float(rows * tiles * width * (channels // GROUPS))

    def decode_body(*refs):
        decode_kernel(width, entries, tiles, *refs)

    return pl.pallas_call(
        decode_body,
        out_shape=jax.ShapeDtypeStruct((2, rows, width, channels), BF16),
        in_specs=[SMEM] + [VMEM] * 5,
        out_specs=VMEM,
        scratch_shapes=[pltpu.VMEM((4, 4, 3, channels, LANES), BF16)],
        compiler_params=PARAMS,
        name="decode",
    )(lengths, sums, hidden, w_mid_t, norm_gain[:, None], bias_mid[:, None])


def solution(mesh):
    return jax.shard_map(
        body,
        mesh=mesh,
        in_specs=(P("tm", "tile", None), P(), P(), P(), P(), P(), P(), P()),
        out_specs=P("tm", "tile", None, None),
        check_vma=False,
    )
```

```python
import jax
import jax.numpy as jnp
from jax import lax
from jax.experimental import pallas as pl
from jax.experimental.pallas import tpu as pltpu
from jax.sharding import PartitionSpec as P

GROUPS = 32
LANES = 256
EARLY = 13
VMEM = pl.BlockSpec(memory_space=pltpu.VMEM)
SMEM = pl.BlockSpec(memory_space=pltpu.SMEM)
HBM = pl.BlockSpec(memory_space=pltpu.HBM)
F32 = jnp.float32
BF16 = jnp.bfloat16
PARAMS = pltpu.CompilerParams(vmem_limit_bytes=40 * 1024 * 1024)


def roll_both(v, axis):
    return pltpu.roll(v, 1, axis), pltpu.roll(v, v.shape[axis] - 1, axis)


def split3(x):
    a = x.astype(BF16).astype(F32)
    b = (x - a).astype(BF16).astype(F32)
    return [a, b, (x - a - b).astype(BF16).astype(F32)]


def pick_kernel(zc, frames, whole_ref, gathered_ref, picked_ref, flags_ref, raw_ref):
    first = 2 * lax.axis_index("tm")
    base = first - 4
    raw_ref[...] = jnp.zeros_like(raw_ref)

    @pl.loop(0, frames)
    def _(p):
        j = whole_ref[p] - base

        @pl.when((j >= 0) & (j < 6))
        def _():
            raw_ref[j] = gathered_ref[p].astype(F32)

    row = lax.broadcasted_iota(jnp.int32, (16, 128), 0)
    lane = lax.broadcasted_iota(jnp.int32, (16, 128), 1)
    channel = jnp.where(lax.rem(lane, zc) == row, 1.0, 0.0).astype(BF16)
    own = lane // zc == lax.rem(row, 128 // zc)
    rows, cells = raw_ref.shape[1:]
    empty = jnp.zeros((LANES - cells // zc, 128), BF16)
    for f in range(6):
        for r in range(rows):
            blocks = []
            for b in range(0, cells, 256):
                halves = [
                    jnp.broadcast_to(raw_ref[f, r : r + 1, b + d : b + d + 128], (128 // zc, 128)) for d in (0, 128)
                ]
                blocks.append(jnp.where(own, jnp.concatenate(halves, axis=0), 0.0).astype(BF16))
            spread_out = jnp.concatenate(blocks + [empty], axis=0)
            picked_ref[f, r] = lax.dot_general(
                channel, spread_out, (((1,), (1,)), ((), ())), preferred_element_type=F32
            ).astype(BF16)

    for j in range(4):
        frame = first - 2 + j
        begin = jnp.int32(0)
        end = jnp.int32(0)
        for r in range(frames, whole_ref.shape[0]):
            end = end + whole_ref[r]
            begin = jnp.where(end <= frame, end, begin)
        for k in range(2):
            flag = jnp.where(frame - 2 + k >= begin, 1.0, 0.0).astype(F32)
            flags_ref[2 * j + k : 2 * j + k + 1, :] = jnp.full((1, LANES), flag, F32)


def group_mask(channels, frame):
    per_group = channels // GROUPS
    channel = lax.broadcasted_iota(jnp.int32, (channels, 128), 0)
    lane = lax.broadcasted_iota(jnp.int32, (channels, 128), 1) - GROUPS * frame
    low = lane * per_group
    return (channel >= low) & (channel < low + per_group) & (lane >= 0) & (lane < GROUPS)


def spread(xs_ref, f, e, v):
    left, right = roll_both(v.astype(F32), 1)
    xs_ref[f, e, 0:16] = left.astype(BF16)
    xs_ref[f, e, 16:32] = v
    xs_ref[f, e, 32:48] = right.astype(BF16)


def frame_weights(w_ref, flags_ref):
    channels = w_ref.shape[1]
    taps = w_ref.shape[0] - 8
    parts = [w_ref[:taps]] + split3(w_ref[taps : taps + 1]) + [jnp.zeros((13, channels), F32)]
    whole = jnp.concatenate(parts, axis=0).T
    lane = lax.broadcasted_iota(jnp.int32, (1, whole.shape[1]), 1)
    result = []
    for j in range(4):
        u0 = flags_ref[2 * j : 2 * j + 1, 0:1]
        u1 = flags_ref[2 * j + 1 : 2 * j + 2, 0:1]
        keep = jnp.where(lane < 144, u0, jnp.where(lane < 288, u1, 1.0))
        result.append((whole * keep).astype(BF16))
    return result


def hidden_t(weights, xs_ref, j, r):
    patches = [xs_ref[j + k, r : r + 3].reshape(144, LANES) for k in range(3)]
    patches.append(jnp.ones((16, LANES), BF16))
    return jnp.dot(weights, jnp.concatenate(patches, axis=0), preferred_element_type=F32)


def sums_kernel(width, tiles, flags_ref, above_ref, picked_ref, w_ref, sums_ref, xs_ref, s1_ref, s2_ref):
    channels = w_ref.shape[1]
    tile = lax.axis_index("tile")
    for f in range(6):
        for e in range(4):
            spread(xs_ref, f, e, (above_ref, picked_ref)[e // 2][f, e % 2])
        xs_ref[f, 4] = jnp.zeros((48, LANES), BF16)
    weights = frame_weights(w_ref, flags_ref)
    lane = lax.broadcasted_iota(jnp.int32, (channels, LANES), 1)
    limit = jnp.where(tile > 0, width, 0)

    def row(j, r):
        h = hidden_t(weights[j], xs_ref, j, r)
        h = jnp.where(lane < (limit if r == 0 else width), h.astype(BF16).astype(F32), 0.0)
        return h[:, :128] + h[:, 128:], h[:, :128] * h[:, :128] + h[:, 128:] * h[:, 128:]

    for j in range(4):
        a1, a2 = row(j, 0)
        b1, b2 = row(j, 1)
        s1_ref[j] = a1 + b1
        s2_ref[j] = a2 + b2

    @pl.when(tile == tiles - 1)
    def _():
        for j in range(4):
            c1, c2 = row(j, 2)
            s1_ref[j] = s1_ref[j] + c1
            s2_ref[j] = s2_ref[j] + c2

    d1 = jnp.zeros((channels, 128), F32)
    d2 = jnp.zeros((channels, 128), F32)
    for j in range(4):
        mask = group_mask(channels, j)
        d1 = jnp.where(mask, jnp.sum(s1_ref[j], axis=1, keepdims=True), d1)
        d2 = jnp.where(mask, jnp.sum(s2_ref[j], axis=1, keepdims=True), d2)
    block = jnp.concatenate([jnp.sum(d1, axis=0, keepdims=True), jnp.sum(d2, axis=0, keepdims=True)], axis=0)
    sums_ref[...] = jnp.broadcast_to(block[None], sums_ref.shape)


def hidden_kernel(
    width, flags_ref, above_ref, picked_ref, below_ref, w_ref, w_mid_hbm, hidden_ref, early_ref, xs_ref, sem
):
    fetch = pltpu.make_async_copy(w_mid_hbm.at[0:EARLY], early_ref, sem)
    fetch.start()
    for f in range(6):
        for e in range(6):
            spread(xs_ref, f, e, (above_ref, picked_ref, below_ref)[e // 2][f, e % 2])
    weights = frame_weights(w_ref, flags_ref)
    for j in range(4):
        for r in range(4):
            hidden_ref[j, r] = hidden_t(weights[j], xs_ref, j, r).T[:width].astype(BF16)
    fetch.wait()


def decode_kernel(
    entries, tiles, flags_ref, sums_ref, h_ref, early_ref, w_hbm, gain_ref, bias_ref, out_ref, act_ref, acc_ref, late_ref, sem
):
    middle = pltpu.make_async_copy(w_hbm.at[EARLY:18], late_ref.at[0 : 18 - EARLY], sem.at[0])
    last = pltpu.make_async_copy(w_hbm.at[18:27], late_ref.at[18 - EARLY : 27 - EARLY], sem.at[1])
    middle.start()
    last.start()
    width, channels = h_ref.shape[2:]
    per_group = channels // GROUPS
    tile = lax.axis_index("tile")
    total = jnp.sum(sums_ref[...], axis=0)
    average = total[0:1] / entries
    variance = total[1:2] / entries - average * average
    rstd = lax.rsqrt(variance + 1e-06)
    packed = jnp.concatenate(split3(average) + split3(rstd) + [jnp.zeros((2, 128), F32)], axis=0).astype(BF16)
    source = lax.broadcasted_iota(jnp.int32, (128, LANES), 0)
    channel = lax.broadcasted_iota(jnp.int32, (128, LANES), 1)
    position = lax.broadcasted_iota(jnp.int32, (width, channels), 0)
    half_gain = 0.5 * gain_ref[...]
    bias = bias_ref[...]
    for j in range(4):
        start = per_group * (source - GROUPS * j)
        expand = (channel >= start) & (channel < start + per_group) & (source >= GROUPS * j) & (source < GROUPS * (j + 1))
        wide = jnp.dot(packed, jnp.where(expand, 1.0, 0.0).astype(BF16), preferred_element_type=F32)
        mean = (wide[0:1] + wide[1:2] + wide[2:3])[:, :channels]
        scale = (wide[3:4] + wide[4:5] + wide[5:6])[:, :channels] * half_gain
        for r in range(4):
            u = (h_ref[j, r].astype(F32) - mean) * scale
            a = u + u * jnp.tanh(u)
            if r == 0:
                a = jnp.where(tile > 0, a, 0.0)
            if r == 3:
                a = jnp.where(tile < tiles - 1, a, 0.0)
            left, right = roll_both(a, 0)
            act_ref[j, r, 0] = jnp.where(position > 0, left, 0.0).astype(BF16)
            act_ref[j, r, 1] = a.astype(BF16)
            act_ref[j, r, 2] = jnp.where(position < width - 1, right, 0.0).astype(BF16)
        for i in range(2):
            k = j - i
            if k < 0 or k > 2:
                continue
            if i == 0 and k > 0:
                (middle if k == 1 else last).wait()
            taps = [early_ref[t] if t < EARLY else late_ref[t - EARLY] for t in range(9 * k, 9 * k + 9)]
            for r in range(2):
                term = None
                for dy in range(3):
                    for dx in range(3):
                        d = jnp.dot(act_ref[j, r + dy, dx], taps[3 * dy + dx], preferred_element_type=F32)
                        term = d if term is None else term + d
                if k < 2:
                    flag = flags_ref[2 * (i + 2) + k : 2 * (i + 2) + k + 1, :channels]
                    term = jnp.where(flag > 0.0, term, 0.0)
                if k == 0:
                    acc_ref[i, r] = term
                elif k == 1:
                    acc_ref[i, r] = acc_ref[i, r] + term
                else:
                    y = acc_ref[i, r] + term + bias + h_ref[2 + i, r + 1].astype(F32)
                    out_ref[i, r] = y.astype(BF16)


def body(latents, frame_slot, lengths, w_in, bias_in, norm_gain, w_mid, bias_mid):
    rows = latents.shape[1]
    zc = w_in.shape[0]
    channels = w_in.shape[2]
    width = latents.shape[2] // zc
    tiles = lax.axis_size("tile")
    whole = jnp.concatenate([frame_slot, lengths])
    latents, whole = lax.optimization_barrier((latents, whole))
    gathered = lax.all_gather(latents, "tm", axis=0, tiled=True)

    def pick_body(*refs):
        pick_kernel(zc, frame_slot.shape[0], *refs)

    picked, flags = pl.pallas_call(
        pick_body,
        out_shape=[jax.ShapeDtypeStruct((6, rows, zc, LANES), BF16), jax.ShapeDtypeStruct((8, LANES), F32)],
        in_specs=[SMEM, VMEM],
        out_specs=[VMEM, VMEM],
        scratch_shapes=[
            pltpu.VMEM((6,) + latents.shape[1:], F32),
        ],
        compiler_params=PARAMS,
        name="pick",
    )(whole, gathered)
    above = lax.ppermute(picked, "tile", [(i, i + 1) for i in range(tiles - 1)])
    below = lax.ppermute(picked, "tile", [(i + 1, i) for i in range(tiles - 1)])
    w_in = jnp.transpose(w_in, (1, 0, 2)).reshape(27 * zc, channels).astype(F32)
    w_in = jnp.concatenate([w_in, jnp.broadcast_to(bias_in[None], (8, channels))], axis=0)
    w_mid = jnp.transpose(w_mid, (1, 0, 2))

    def sums_body(*refs):
        sums_kernel(width, tiles, *refs)

    def hidden_body(*refs):
        hidden_kernel(width, *refs)

    sums = pl.pallas_call(
        sums_body,
        out_shape=jax.ShapeDtypeStruct((tiles, 2, 128), F32),
        in_specs=[VMEM] * 4,
        out_specs=VMEM,
        scratch_shapes=[
            pltpu.VMEM((6, 5, 3 * zc, LANES), BF16),
            pltpu.VMEM((4, channels, 128), F32),
            pltpu.VMEM((4, channels, 128), F32),
        ],
        compiler_params=PARAMS,
        name="sums",
    )(flags, above, picked, w_in)
    sums = lax.all_to_all(sums, "tile", 0, 0)
    hidden, early = pl.pallas_call(
        hidden_body,
        out_shape=[
            jax.ShapeDtypeStruct((4, 4, width, channels), BF16),
            jax.ShapeDtypeStruct((EARLY, channels, channels), BF16),
        ],
        in_specs=[VMEM] * 5 + [HBM],
        out_specs=[VMEM, VMEM],
        scratch_shapes=[
            pltpu.VMEM((6, 6, 3 * zc, LANES), BF16),
            pltpu.SemaphoreType.DMA,
        ],
        compiler_params=pltpu.CompilerParams(vmem_limit_bytes=50000 * 1024),
        cost_estimate=pl.CostEstimate(flops=4_000_000_000, bytes_accessed=2_000_000, transcendentals=0),
        name="hidden",
    )(flags, above, picked, below, w_in, w_mid)
    entries = float(rows * tiles * width * (channels // GROUPS))

    def decode_body(*refs):
        decode_kernel(entries, tiles, *refs)

    return pl.pallas_call(
        decode_body,
        out_shape=jax.ShapeDtypeStruct((2, rows, width, channels), BF16),
        in_specs=[VMEM, VMEM, VMEM, VMEM, HBM, VMEM, VMEM],
        out_specs=VMEM,
        scratch_shapes=[
            pltpu.VMEM((4, 4, 3, width, channels), BF16),
            pltpu.VMEM((2, 2, width, channels), F32),
            pltpu.VMEM((27 - EARLY, channels, channels), BF16),
            pltpu.SemaphoreType.DMA((2,)),
        ],
        compiler_params=pltpu.CompilerParams(vmem_limit_bytes=52000 * 1024),
        name="decode",
    )(flags, sums, hidden, early, w_mid, norm_gain[None, :], bias_mid[None, :])


def solution(mesh):
    return jax.shard_map(
        body,
        mesh=mesh,
        in_specs=(P("tm", "tile", None), P(), P(), P(), P(), P(), P(), P()),
        out_specs=P("tm", "tile", None, None),
        check_vma=False,
    )
```

```python
import jax
import jax.numpy as jnp
from jax import lax
from jax.experimental import pallas as pl
from jax.experimental.pallas import tpu as pltpu
from jax.sharding import PartitionSpec as P

GROUPS = 32
LANES = 256
EARLY = 13
TIMES = list(range(15, -1, -1))
TILES = [8 * x + z for z in (4, 5, 6, 7, 3, 2, 1, 0) for x in (2, 3, 1, 0)]
VMEM = pl.BlockSpec(memory_space=pltpu.VMEM)
SMEM = pl.BlockSpec(memory_space=pltpu.SMEM)
HBM = pl.BlockSpec(memory_space=pltpu.HBM)
F32 = jnp.float32
BF16 = jnp.bfloat16
PARAMS = pltpu.CompilerParams(vmem_limit_bytes=40 * 1024 * 1024)


def roll_both(v, axis):
    return pltpu.roll(v, 1, axis), pltpu.roll(v, v.shape[axis] - 1, axis)


def split3(x):
    a = x.astype(BF16).astype(F32)
    b = (x - a).astype(BF16).astype(F32)
    return [a, b, (x - a - b).astype(BF16).astype(F32)]


def pick_kernel(zc, frames, whole_ref, gathered_ref, picked_ref, flags_ref, where_ref, raw_ref):
    first = 2 * lax.axis_index("tm")
    for p in range(frames):
        where_ref[whole_ref[p]] = 2 * TIMES.index(p // 2) + p % 2
    for j in range(6):
        t = first - 4 + j
        raw = gathered_ref[where_ref[jnp.maximum(t, 0)]].astype(F32)
        raw_ref[j] = raw if j > 3 else jnp.where(t >= 0, raw, 0.0)
    row = lax.broadcasted_iota(jnp.int32, (16, 128), 0)
    lane = lax.broadcasted_iota(jnp.int32, (16, 128), 1)
    channel = jnp.where(lax.rem(lane, zc) == row, 1.0, 0.0).astype(BF16)
    own = lane // zc == lax.rem(row, 128 // zc)
    rows, cells = raw_ref.shape[1:]
    empty = jnp.zeros((LANES - cells // zc, 128), BF16)
    for f in range(6):
        for r in range(rows):
            blocks = []
            for b in range(0, cells, 256):
                halves = [
                    jnp.broadcast_to(raw_ref[f, r : r + 1, b + d : b + d + 128], (128 // zc, 128)) for d in (0, 128)
                ]
                blocks.append(jnp.where(own, jnp.concatenate(halves, axis=0), 0.0).astype(BF16))
            spread_out = jnp.concatenate(blocks + [empty], axis=0)
            picked_ref[f, r] = lax.dot_general(
                channel, spread_out, (((1,), (1,)), ((), ())), preferred_element_type=F32
            ).astype(BF16)

    for j in range(4):
        frame = first - 2 + j
        begin = jnp.int32(0)
        end = jnp.int32(0)
        for r in range(frames, whole_ref.shape[0]):
            end = end + whole_ref[r]
            begin = jnp.where(end <= frame, end, begin)
        for k in range(2):
            flag = jnp.where(frame - 2 + k >= begin, 1.0, 0.0).astype(F32)
            flags_ref[2 * j + k : 2 * j + k + 1, :] = jnp.full((1, LANES), flag, F32)


def group_mask(channels, frame):
    per_group = channels // GROUPS
    channel = lax.broadcasted_iota(jnp.int32, (channels, 128), 0)
    lane = lax.broadcasted_iota(jnp.int32, (channels, 128), 1) - GROUPS * frame
    low = lane * per_group
    return (channel >= low) & (channel < low + per_group) & (lane >= 0) & (lane < GROUPS)


def spread(xs_ref, f, e, v):
    left, right = roll_both(v.astype(F32), 1)
    xs_ref[f, e, 0:16] = left.astype(BF16)
    xs_ref[f, e, 16:32] = v
    xs_ref[f, e, 32:48] = right.astype(BF16)


def frame_weights(w_ref, flags_ref):
    taps = w_ref.shape[1] - 8
    whole = w_ref[:, :taps].astype(BF16)
    lane = lax.broadcasted_iota(jnp.int32, (1, taps), 1)
    result = []
    for j in range(4):
        u0 = flags_ref[2 * j : 2 * j + 1, 0:1]
        u1 = flags_ref[2 * j + 1 : 2 * j + 2, 0:1]
        keep = jnp.where(lane < taps // 3, u0, jnp.where(lane < 2 * taps // 3, u1, 1.0)).astype(BF16)
        result.append(whole * keep)
    return result, w_ref[:, taps : taps + 1]


def hidden_t(weights, bias, xs_ref, j, r):
    patches = jnp.concatenate([xs_ref[j + k, r : r + 3].reshape(144, LANES) for k in range(3)], axis=0)
    return jnp.dot(weights, patches, preferred_element_type=F32) + bias


def sums_kernel(width, tiles, flags_ref, above_ref, picked_ref, w_ref, sums_ref, xs_ref, s1_ref, s2_ref):
    channels = w_ref.shape[0]
    tile = lax.axis_index("tile")
    for f in range(6):
        for e in range(4):
            spread(xs_ref, f, e, (above_ref, picked_ref)[e // 2][f, e % 2])
        xs_ref[f, 4] = jnp.zeros((48, LANES), BF16)
    weights, bias = frame_weights(w_ref, flags_ref)
    rest = lax.broadcasted_iota(jnp.int32, (channels, 128), 1) < width - 128

    def row(j, r):
        h = hidden_t(weights[j], bias, xs_ref, j, r).astype(BF16).astype(F32)
        a, b = h[:, :128], jnp.where(rest, h[:, 128:], 0.0)
        if r == 0:
            a, b = jnp.where(tile > 0, a, 0.0), jnp.where(tile > 0, b, 0.0)
        return a + b, a * a + b * b

    for j in range(4):
        a1, a2 = row(j, 0)
        b1, b2 = row(j, 1)
        s1_ref[j] = a1 + b1
        s2_ref[j] = a2 + b2

    @pl.when(tile == tiles - 1)
    def _():
        for j in range(4):
            c1, c2 = row(j, 2)
            s1_ref[j] = s1_ref[j] + c1
            s2_ref[j] = s2_ref[j] + c2

    d1 = jnp.zeros((channels, 128), F32)
    d2 = jnp.zeros((channels, 128), F32)
    for j in range(4):
        mask = group_mask(channels, j)
        d1 = jnp.where(mask, jnp.sum(s1_ref[j], axis=1, keepdims=True), d1)
        d2 = jnp.where(mask, jnp.sum(s2_ref[j], axis=1, keepdims=True), d2)
    block = jnp.concatenate([jnp.sum(d1, axis=0, keepdims=True), jnp.sum(d2, axis=0, keepdims=True)], axis=0)
    sums_ref[...] = jnp.broadcast_to(block[None], sums_ref.shape)


def hidden_kernel(
    width, flags_ref, above_ref, picked_ref, below_ref, w_ref, w_mid_hbm, hidden_ref, early_ref, xs_ref, sem
):
    fetch = pltpu.make_async_copy(w_mid_hbm.at[0:EARLY], early_ref, sem)
    fetch.start()
    for f in range(6):
        for e in range(6):
            spread(xs_ref, f, e, (above_ref, picked_ref, below_ref)[e // 2][f, e % 2])
    weights, bias = frame_weights(w_ref, flags_ref)
    for j in range(4):
        for r in range(4):
            hidden_ref[j, r] = hidden_t(weights[j], bias, xs_ref, j, r).T[:width].astype(BF16)
    fetch.wait()


def decode_kernel(
    entries, tiles, flags_ref, sums_ref, h_ref, early_ref, w_hbm, gain_ref, bias_ref, out_hbm, act_ref, acc_ref, late_ref, out_ref, sem, out_sem
):
    late = pltpu.make_async_copy(w_hbm.at[EARLY:27], late_ref, sem)
    late.start()
    width, channels = h_ref.shape[2:]
    per_group = channels // GROUPS
    tile = lax.axis_index("tile")
    total = jnp.sum(sums_ref[...], axis=0)
    average = total[0:1] / entries
    variance = total[1:2] / entries - average * average
    rstd = lax.rsqrt(variance + 1e-06)
    packed = jnp.concatenate(split3(average) + split3(rstd) + [jnp.zeros((2, 128), F32)], axis=0).astype(BF16)
    source = lax.broadcasted_iota(jnp.int32, (128, LANES), 0)
    channel = lax.broadcasted_iota(jnp.int32, (128, LANES), 1)
    position = lax.broadcasted_iota(jnp.int32, (width, channels), 0)
    half_gain = 0.5 * gain_ref[...]
    results = []
    bias = bias_ref[...]

    def activate(j):
        start = per_group * (source - GROUPS * j)
        expand = (channel >= start) & (channel < start + per_group) & (source >= GROUPS * j) & (source < GROUPS * (j + 1))
        wide = jnp.dot(packed, jnp.where(expand, 1.0, 0.0).astype(BF16), preferred_element_type=F32)
        mean = (wide[0:1] + wide[1:2] + wide[2:3])[:, :channels]
        scale = (wide[3:4] + wide[4:5] + wide[5:6])[:, :channels] * half_gain
        for r in range(4):
            u = (h_ref[j, r].astype(F32) - mean) * scale
            a = u + u * jnp.tanh(u)
            if r == 0:
                a = jnp.where(tile > 0, a, 0.0)
            if r == 3:
                a = jnp.where(tile < tiles - 1, a, 0.0)
            left, right = roll_both(a, 0)
            act_ref[j, r, 0] = jnp.where(position > 0, left, 0.0).astype(BF16)
            act_ref[j, r, 1] = a.astype(BF16)
            act_ref[j, r, 2] = jnp.where(position < width - 1, right, 0.0).astype(BF16)

    def convolve(i, k):
        taps = [early_ref[t] if t < EARLY else late_ref[t - EARLY] for t in range(9 * k, 9 * k + 9)]
        for r in range(2):
            term = None
            for dy in range(3):
                for dx in range(3):
                    d = jnp.dot(act_ref[i + k, r + dy, dx], taps[3 * dy + dx], preferred_element_type=F32)
                    term = d if term is None else term + d
            if k < 2:
                flag = flags_ref[2 * (i + 2) + k : 2 * (i + 2) + k + 1, :channels]
                term = jnp.where(flag > 0.0, term, 0.0)
            if k == 0:
                acc_ref[i, r] = term
            elif k == 1:
                acc_ref[i, r] = acc_ref[i, r] + term
            else:
                y = acc_ref[i, r] + term + bias + h_ref[2 + i, r + 1].astype(F32)
                out_ref[i, r] = y.astype(BF16)
                results.append(pltpu.make_async_copy(out_ref.at[i, r], out_hbm.at[i, r], out_sem.at[i, r]))
                results[-1].start()

    activate(0)
    convolve(0, 0)
    activate(1)
    convolve(1, 0)
    activate(2)
    late.wait()
    convolve(0, 1)
    convolve(1, 1)
    activate(3)
    convolve(0, 2)
    convolve(1, 2)
    for copy in results:
        copy.wait()


def body(latents, frame_slot, lengths, w_in, bias_in, norm_gain, w_mid, bias_mid):
    rows = latents.shape[1]
    zc = w_in.shape[0]
    channels = w_in.shape[2]
    width = latents.shape[2] // zc
    tiles = lax.axis_size("tile")
    whole = jnp.concatenate([frame_slot, lengths])
    latents, whole = lax.optimization_barrier((latents, whole))
    gathered = lax.all_gather(latents, "tm", axis=0, tiled=True, axis_index_groups=[TIMES])

    def pick_body(*refs):
        pick_kernel(zc, frame_slot.shape[0], *refs)

    picked, flags = pl.pallas_call(
        pick_body,
        out_shape=[jax.ShapeDtypeStruct((6, rows, zc, LANES), BF16), jax.ShapeDtypeStruct((8, LANES), F32)],
        in_specs=[SMEM, VMEM],
        out_specs=[VMEM, VMEM],
        scratch_shapes=[
            pltpu.SMEM(frame_slot.shape, jnp.int32),
            pltpu.VMEM((6,) + latents.shape[1:], F32),
        ],
        compiler_params=PARAMS,
        name="pick",
    )(whole, gathered)
    above = lax.ppermute(picked, "tile", [(i, i + 1) for i in range(tiles - 1)])
    below = lax.ppermute(picked, "tile", [(i + 1, i) for i in range(tiles - 1)])
    w_in = jnp.transpose(w_in, (1, 0, 2)).reshape(27 * zc, channels).astype(F32)
    w_in = jnp.concatenate([w_in, jnp.broadcast_to(bias_in[None], (8, channels))], axis=0).T
    w_mid = jnp.transpose(w_mid, (1, 0, 2))

    def sums_body(*refs):
        sums_kernel(width, tiles, *refs)

    def hidden_body(*refs):
        hidden_kernel(width, *refs)

    sums = pl.pallas_call(
        sums_body,
        out_shape=jax.ShapeDtypeStruct((tiles, 2, 128), F32),
        in_specs=[VMEM] * 4,
        out_specs=VMEM,
        scratch_shapes=[
            pltpu.VMEM((6, 5, 3 * zc, LANES), BF16),
            pltpu.VMEM((4, channels, 128), F32),
            pltpu.VMEM((4, channels, 128), F32),
        ],
        compiler_params=PARAMS,
        name="sums",
    )(flags, above, picked, w_in)
    sums = lax.all_to_all(sums, "tile", 0, 0, axis_index_groups=[TILES])
    hidden, early = pl.pallas_call(
        hidden_body,
        out_shape=[
            jax.ShapeDtypeStruct((4, 4, width, channels), BF16),
            jax.ShapeDtypeStruct((EARLY, channels, channels), BF16),
        ],
        in_specs=[VMEM] * 5 + [HBM],
        out_specs=[VMEM, VMEM],
        scratch_shapes=[
            pltpu.VMEM((6, 6, 3 * zc, LANES), BF16),
            pltpu.SemaphoreType.DMA,
        ],
        compiler_params=pltpu.CompilerParams(vmem_limit_bytes=50000 * 1024),
        cost_estimate=pl.CostEstimate(flops=4_000_000_000, bytes_accessed=2_000_000, transcendentals=0),
        name="hidden",
    )(flags, above, picked, below, w_in, w_mid)
    entries = float(rows * tiles * width * (channels // GROUPS))

    def decode_body(*refs):
        decode_kernel(entries, tiles, *refs)

    return pl.pallas_call(
        decode_body,
        out_shape=jax.ShapeDtypeStruct((2, rows, width, channels), BF16),
        in_specs=[VMEM, VMEM, VMEM, VMEM, HBM, VMEM, VMEM],
        out_specs=HBM,
        scratch_shapes=[
            pltpu.VMEM((4, 4, 3, width, channels), BF16),
            pltpu.VMEM((2, 2, width, channels), F32),
            pltpu.VMEM((27 - EARLY, channels, channels), BF16),
            pltpu.VMEM((2, 2, width, channels), BF16),
            pltpu.SemaphoreType.DMA,
            pltpu.SemaphoreType.DMA((2, 2)),
        ],
        compiler_params=pltpu.CompilerParams(vmem_limit_bytes=52000 * 1024),
        name="decode",
    )(flags, sums, hidden, early, w_mid, norm_gain[None, :], bias_mid[None, :])


def solution(mesh):
    return jax.shard_map(
        body,
        mesh=mesh,
        in_specs=(P("tm", "tile", None), P(), P(), P(), P(), P(), P(), P()),
        out_specs=P("tm", "tile", None, None),
        check_vma=False,
    )
```

```python
import jax
import jax.numpy as jnp
from jax import lax
from jax.experimental import pallas as pl
from jax.experimental.pallas import tpu as pltpu
from jax.sharding import PartitionSpec as P

GROUPS = 32
LANES = 256
EARLY = 13
CHIPS = [5, 6, 7, 4, 3, 2, 1, 0]
TILES = [8 * x + z for z in (4, 5, 6, 7, 3, 2, 1, 0) for x in (2, 3, 1, 0)]
VMEM = pl.BlockSpec(memory_space=pltpu.VMEM)
SMEM = pl.BlockSpec(memory_space=pltpu.SMEM)
HBM = pl.BlockSpec(memory_space=pltpu.HBM)
F32 = jnp.float32
BF16 = jnp.bfloat16
PARAMS = pltpu.CompilerParams(vmem_limit_bytes=40 * 1024 * 1024)


def roll_both(v, axis):
    return pltpu.roll(v, 1, axis), pltpu.roll(v, v.shape[axis] - 1, axis)


def split3(x):
    a = x.astype(BF16).astype(F32)
    b = (x - a).astype(BF16).astype(F32)
    return [a, b, (x - a - b).astype(BF16).astype(F32)]


def pick_kernel(zc, frames, whole_ref, gathered_ref, picked_ref, flags_ref, where_ref, raw_ref):
    first = 2 * lax.axis_index("tm")
    for p in range(frames):
        where_ref[whole_ref[p]] = 16 * (p // 2 % 2) + 2 * CHIPS.index(p // 4) + p % 2
    for j in range(6):
        t = first - 4 + j
        raw = gathered_ref[where_ref[jnp.maximum(t, 0)]].astype(F32)
        raw_ref[j] = raw if j > 3 else jnp.where(t >= 0, raw, 0.0)
    row = lax.broadcasted_iota(jnp.int32, (16, 128), 0)
    lane = lax.broadcasted_iota(jnp.int32, (16, 128), 1)
    channel = jnp.where(lax.rem(lane, zc) == row, 1.0, 0.0).astype(BF16)
    own = lane // zc == lax.rem(row, 128 // zc)
    rows, cells = raw_ref.shape[1:]
    empty = jnp.zeros((LANES - cells // zc, 128), BF16)
    for f in range(6):
        for r in range(rows):
            blocks = []
            for b in range(0, cells, 256):
                halves = [
                    jnp.broadcast_to(raw_ref[f, r : r + 1, b + d : b + d + 128], (128 // zc, 128)) for d in (0, 128)
                ]
                blocks.append(jnp.where(own, jnp.concatenate(halves, axis=0), 0.0).astype(BF16))
            spread_out = jnp.concatenate(blocks + [empty], axis=0)
            picked_ref[f, r] = lax.dot_general(
                channel, spread_out, (((1,), (1,)), ((), ())), preferred_element_type=F32
            ).astype(BF16)

    for j in range(4):
        frame = first - 2 + j
        begin = jnp.int32(0)
        end = jnp.int32(0)
        for r in range(frames, whole_ref.shape[0]):
            end = end + whole_ref[r]
            begin = jnp.where(end <= frame, end, begin)
        for k in range(2):
            flag = jnp.where(frame - 2 + k >= begin, 1.0, 0.0).astype(F32)
            flags_ref[2 * j + k : 2 * j + k + 1, :] = jnp.full((1, LANES), flag, F32)


def group_mask(channels, frame):
    per_group = channels // GROUPS
    channel = lax.broadcasted_iota(jnp.int32, (channels, 128), 0)
    lane = lax.broadcasted_iota(jnp.int32, (channels, 128), 1) - GROUPS * frame
    low = lane * per_group
    return (channel >= low) & (channel < low + per_group) & (lane >= 0) & (lane < GROUPS)


def spread(xs_ref, f, e, v):
    left, right = roll_both(v.astype(F32), 1)
    xs_ref[f, e, 0:16] = left.astype(BF16)
    xs_ref[f, e, 16:32] = v
    xs_ref[f, e, 32:48] = right.astype(BF16)


def frame_weights(w_ref, flags_ref):
    taps = w_ref.shape[1] - 8
    whole = w_ref[:, :taps].astype(BF16)
    lane = lax.broadcasted_iota(jnp.int32, (1, taps), 1)
    result = []
    for j in range(4):
        u0 = flags_ref[2 * j : 2 * j + 1, 0:1]
        u1 = flags_ref[2 * j + 1 : 2 * j + 2, 0:1]
        keep = jnp.where(lane < taps // 3, u0, jnp.where(lane < 2 * taps // 3, u1, 1.0)).astype(BF16)
        result.append(whole * keep)
    return result, w_ref[:, taps : taps + 1]


def hidden_t(weights, bias, xs_ref, j, r):
    patches = jnp.concatenate([xs_ref[j + k, r : r + 3].reshape(144, LANES) for k in range(3)], axis=0)
    return jnp.dot(weights, patches, preferred_element_type=F32) + bias


def sums_kernel(width, tiles, flags_ref, above_ref, picked_ref, w_ref, sums_ref, xs_ref, s1_ref, s2_ref):
    channels = w_ref.shape[0]
    tile = lax.axis_index("tile")
    for f in range(6):
        for e in range(4):
            spread(xs_ref, f, e, (above_ref, picked_ref)[e // 2][f, e % 2])
        xs_ref[f, 4] = jnp.zeros((48, LANES), BF16)
    weights, bias = frame_weights(w_ref, flags_ref)
    rest = lax.broadcasted_iota(jnp.int32, (channels, 128), 1) < width - 128

    def row(j, r):
        h = hidden_t(weights[j], bias, xs_ref, j, r).astype(BF16).astype(F32)
        a, b = h[:, :128], jnp.where(rest, h[:, 128:], 0.0)
        if r == 0:
            a, b = jnp.where(tile > 0, a, 0.0), jnp.where(tile > 0, b, 0.0)
        return a + b, a * a + b * b

    for j in range(4):
        a1, a2 = row(j, 0)
        b1, b2 = row(j, 1)
        s1_ref[j] = a1 + b1
        s2_ref[j] = a2 + b2

    @pl.when(tile == tiles - 1)
    def _():
        for j in range(4):
            c1, c2 = row(j, 2)
            s1_ref[j] = s1_ref[j] + c1
            s2_ref[j] = s2_ref[j] + c2

    d1 = jnp.zeros((channels, 128), F32)
    d2 = jnp.zeros((channels, 128), F32)
    for j in range(4):
        mask = group_mask(channels, j)
        d1 = jnp.where(mask, jnp.sum(s1_ref[j], axis=1, keepdims=True), d1)
        d2 = jnp.where(mask, jnp.sum(s2_ref[j], axis=1, keepdims=True), d2)
    block = jnp.concatenate([jnp.sum(d1, axis=0, keepdims=True), jnp.sum(d2, axis=0, keepdims=True)], axis=0)
    sums_ref[...] = jnp.broadcast_to(block[None], sums_ref.shape)


def hidden_kernel(
    width, flags_ref, above_ref, picked_ref, below_ref, w_ref, w_mid_hbm, hidden_ref, early_ref, xs_ref, sem
):
    fetch = pltpu.make_async_copy(w_mid_hbm.at[0:EARLY], early_ref, sem)
    fetch.start()
    for f in range(6):
        for e in range(6):
            spread(xs_ref, f, e, (above_ref, picked_ref, below_ref)[e // 2][f, e % 2])
    weights, bias = frame_weights(w_ref, flags_ref)
    for j in range(4):
        for r in range(4):
            hidden_ref[j, r] = hidden_t(weights[j], bias, xs_ref, j, r).T[:width].astype(BF16)
    fetch.wait()


def decode_kernel(
    entries, tiles, flags_ref, sums_ref, h_ref, early_ref, w_hbm, gain_ref, bias_ref, out_hbm, act_ref, acc_ref, late_ref, out_ref, sem, out_sem
):
    late = pltpu.make_async_copy(w_hbm.at[EARLY:27], late_ref, sem)
    late.start()
    width, channels = h_ref.shape[2:]
    per_group = channels // GROUPS
    tile = lax.axis_index("tile")
    total = jnp.sum(sums_ref[...], axis=0)
    average = total[0:1] / entries
    variance = total[1:2] / entries - average * average
    rstd = lax.rsqrt(variance + 1e-06)
    packed = jnp.concatenate(split3(average) + split3(rstd) + [jnp.zeros((2, 128), F32)], axis=0).astype(BF16)
    source = lax.broadcasted_iota(jnp.int32, (128, LANES), 0)
    channel = lax.broadcasted_iota(jnp.int32, (128, LANES), 1)
    position = lax.broadcasted_iota(jnp.int32, (width, channels), 0)
    half_gain = 0.5 * gain_ref[...]
    results = []
    bias = bias_ref[...]

    def activate(j):
        start = per_group * (source - GROUPS * j)
        expand = (channel >= start) & (channel < start + per_group) & (source >= GROUPS * j) & (source < GROUPS * (j + 1))
        wide = jnp.dot(packed, jnp.where(expand, 1.0, 0.0).astype(BF16), preferred_element_type=F32)
        mean = (wide[0:1] + wide[1:2] + wide[2:3])[:, :channels]
        scale = (wide[3:4] + wide[4:5] + wide[5:6])[:, :channels] * half_gain
        for r in range(4):
            u = (h_ref[j, r].astype(F32) - mean) * scale
            a = u + u * jnp.tanh(u)
            if r == 0:
                a = jnp.where(tile > 0, a, 0.0)
            if r == 3:
                a = jnp.where(tile < tiles - 1, a, 0.0)
            left, right = roll_both(a, 0)
            act_ref[j, r, 0] = jnp.where(position > 0, left, 0.0).astype(BF16)
            act_ref[j, r, 1] = a.astype(BF16)
            act_ref[j, r, 2] = jnp.where(position < width - 1, right, 0.0).astype(BF16)

    def convolve(i, k):
        taps = [early_ref[t] if t < EARLY else late_ref[t - EARLY] for t in range(9 * k, 9 * k + 9)]
        for r in range(2):
            term = None
            for dy in range(3):
                for dx in range(3):
                    d = jnp.dot(act_ref[i + k, r + dy, dx], taps[3 * dy + dx], preferred_element_type=F32)
                    term = d if term is None else term + d
            if k < 2:
                flag = flags_ref[2 * (i + 2) + k : 2 * (i + 2) + k + 1, :channels]
                term = jnp.where(flag > 0.0, term, 0.0)
            if k == 0:
                acc_ref[i, r] = term
            elif k == 1:
                acc_ref[i, r] = acc_ref[i, r] + term
            else:
                y = acc_ref[i, r] + term + bias + h_ref[2 + i, r + 1].astype(F32)
                out_ref[i, r] = y.astype(BF16)
                results.append(pltpu.make_async_copy(out_ref.at[i, r], out_hbm.at[i, r], out_sem.at[i, r]))
                results[-1].start()

    activate(0)
    convolve(0, 0)
    activate(1)
    convolve(1, 0)
    activate(2)
    late.wait()
    convolve(0, 1)
    convolve(1, 1)
    activate(3)
    convolve(0, 2)
    convolve(1, 2)
    for copy in results:
        copy.wait()


def body(latents, frame_slot, lengths, w_in, bias_in, norm_gain, w_mid, bias_mid):
    rows = latents.shape[1]
    zc = w_in.shape[0]
    channels = w_in.shape[2]
    width = latents.shape[2] // zc
    tiles = lax.axis_size("tile")
    whole = jnp.concatenate([frame_slot, lengths])
    cores = [[2 * y + c for y in CHIPS] for c in range(2)]
    column = lax.all_to_all(jnp.broadcast_to(latents[None], (8,) + latents.shape), "tm", 0, 0, axis_index_groups=cores)
    gathered = lax.all_gather(column, "tm", axis=0, axis_index_groups=[[2 * y, 2 * y + 1] for y in range(8)])
    gathered = gathered.reshape((32,) + latents.shape[1:])

    def pick_body(*refs):
        pick_kernel(zc, frame_slot.shape[0], *refs)

    picked, flags = pl.pallas_call(
        pick_body,
        out_shape=[jax.ShapeDtypeStruct((6, rows, zc, LANES), BF16), jax.ShapeDtypeStruct((8, LANES), F32)],
        in_specs=[SMEM, VMEM],
        out_specs=[VMEM, VMEM],
        scratch_shapes=[
            pltpu.SMEM(frame_slot.shape, jnp.int32),
            pltpu.VMEM((6,) + latents.shape[1:], F32),
        ],
        compiler_params=PARAMS,
        name="pick",
    )(whole, gathered)
    above = lax.ppermute(picked, "tile", [(i, i + 1) for i in range(tiles - 1)])
    below = lax.ppermute(picked, "tile", [(i + 1, i) for i in range(tiles - 1)])
    w_in = jnp.transpose(w_in, (1, 0, 2)).reshape(27 * zc, channels).astype(F32)
    w_in = jnp.concatenate([w_in, jnp.broadcast_to(bias_in[None], (8, channels))], axis=0).T
    w_mid = jnp.transpose(w_mid, (1, 0, 2))

    def sums_body(*refs):
        sums_kernel(width, tiles, *refs)

    def hidden_body(*refs):
        hidden_kernel(width, *refs)

    sums = pl.pallas_call(
        sums_body,
        out_shape=jax.ShapeDtypeStruct((tiles, 2, 128), F32),
        in_specs=[VMEM] * 4,
        out_specs=VMEM,
        scratch_shapes=[
            pltpu.VMEM((6, 5, 3 * zc, LANES), BF16),
            pltpu.VMEM((4, channels, 128), F32),
            pltpu.VMEM((4, channels, 128), F32),
        ],
        compiler_params=PARAMS,
        name="sums",
    )(flags, above, picked, w_in)
    sums = lax.all_to_all(sums, "tile", 0, 0, axis_index_groups=[TILES])
    hidden, early = pl.pallas_call(
        hidden_body,
        out_shape=[
            jax.ShapeDtypeStruct((4, 4, width, channels), BF16),
            jax.ShapeDtypeStruct((EARLY, channels, channels), BF16),
        ],
        in_specs=[VMEM] * 5 + [HBM],
        out_specs=[VMEM, VMEM],
        scratch_shapes=[
            pltpu.VMEM((6, 6, 3 * zc, LANES), BF16),
            pltpu.SemaphoreType.DMA,
        ],
        compiler_params=pltpu.CompilerParams(vmem_limit_bytes=50000 * 1024),
        cost_estimate=pl.CostEstimate(flops=4_000_000_000, bytes_accessed=2_000_000, transcendentals=0),
        name="hidden",
    )(flags, above, picked, below, w_in, w_mid)
    entries = float(rows * tiles * width * (channels // GROUPS))

    def decode_body(*refs):
        decode_kernel(entries, tiles, *refs)

    return pl.pallas_call(
        decode_body,
        out_shape=jax.ShapeDtypeStruct((2, rows, width, channels), BF16),
        in_specs=[VMEM, VMEM, VMEM, VMEM, HBM, VMEM, VMEM],
        out_specs=HBM,
        scratch_shapes=[
            pltpu.VMEM((4, 4, 3, width, channels), BF16),
            pltpu.VMEM((2, 2, width, channels), F32),
            pltpu.VMEM((27 - EARLY, channels, channels), BF16),
            pltpu.VMEM((2, 2, width, channels), BF16),
            pltpu.SemaphoreType.DMA,
            pltpu.SemaphoreType.DMA((2, 2)),
        ],
        compiler_params=pltpu.CompilerParams(vmem_limit_bytes=52000 * 1024),
        name="decode",
    )(flags, sums, hidden, early, w_mid, norm_gain[None, :], bias_mid[None, :])


def solution(mesh):
    return jax.shard_map(
        body,
        mesh=mesh,
        in_specs=(P("tm", "tile", None), P(), P(), P(), P(), P(), P(), P()),
        out_specs=P("tm", "tile", None, None),
        check_vma=False,
    )
```

```python
import jax
import jax.numpy as jnp
from jax import lax
from jax.experimental import pallas as pl
from jax.experimental.pallas import tpu as pltpu
from jax.sharding import PartitionSpec as P

GROUPS = 32
LANES = 256
EARLY = 16
CHIPS = [5, 6, 7, 4, 3, 2, 1, 0]
TILES = [8 * x + z for z in (4, 5, 6, 7, 3, 2, 1, 0) for x in (2, 3, 1, 0)]
VMEM = pl.BlockSpec(memory_space=pltpu.VMEM)
SMEM = pl.BlockSpec(memory_space=pltpu.SMEM)
HBM = pl.BlockSpec(memory_space=pltpu.HBM)
F32 = jnp.float32
BF16 = jnp.bfloat16
PARAMS = pltpu.CompilerParams(vmem_limit_bytes=40 * 1024 * 1024)


def roll_both(v, axis):
    return pltpu.roll(v, 1, axis), pltpu.roll(v, v.shape[axis] - 1, axis)


def split3(x):
    a = x.astype(BF16).astype(F32)
    b = (x - a).astype(BF16).astype(F32)
    return [a, b, (x - a - b).astype(BF16).astype(F32)]


def pick_kernel(zc, frames, whole_ref, gathered_ref, picked_ref, flags_ref, where_ref, raw_ref):
    first = 2 * lax.axis_index("tm")
    for p in range(frames):
        where_ref[whole_ref[p]] = 16 * (p // 2 % 2) + 2 * CHIPS.index(p // 4) + p % 2
    for j in range(6):
        t = first - 4 + j
        raw = gathered_ref[where_ref[jnp.maximum(t, 0)]].astype(F32)
        raw_ref[j] = raw if j > 3 else jnp.where(t >= 0, raw, 0.0)
    row = lax.broadcasted_iota(jnp.int32, (16, 128), 0)
    lane = lax.broadcasted_iota(jnp.int32, (16, 128), 1)
    channel = jnp.where(lax.rem(lane, zc) == row, 1.0, 0.0).astype(BF16)
    own = lane // zc == lax.rem(row, 128 // zc)
    rows, cells = raw_ref.shape[1:]
    empty = jnp.zeros((LANES - cells // zc, 128), BF16)
    for f in range(6):
        for r in range(rows):
            blocks = []
            for b in range(0, cells, 256):
                halves = [
                    jnp.broadcast_to(raw_ref[f, r : r + 1, b + d : b + d + 128], (128 // zc, 128)) for d in (0, 128)
                ]
                blocks.append(jnp.where(own, jnp.concatenate(halves, axis=0), 0.0).astype(BF16))
            spread_out = jnp.concatenate(blocks + [empty], axis=0)
            picked_ref[f, r] = lax.dot_general(
                channel, spread_out, (((1,), (1,)), ((), ())), preferred_element_type=F32
            ).astype(BF16)

    for j in range(4):
        frame = first - 2 + j
        begin = jnp.int32(0)
        end = jnp.int32(0)
        for r in range(frames, whole_ref.shape[0]):
            end = end + whole_ref[r]
            begin = jnp.where(end <= frame, end, begin)
        for k in range(2):
            flag = jnp.where(frame - 2 + k >= begin, 1.0, 0.0).astype(F32)
            flags_ref[2 * j + k : 2 * j + k + 1, :] = jnp.full((1, LANES), flag, F32)


def group_mask(channels, frame):
    per_group = channels // GROUPS
    channel = lax.broadcasted_iota(jnp.int32, (channels, 128), 0)
    lane = lax.broadcasted_iota(jnp.int32, (channels, 128), 1) - GROUPS * frame
    low = lane * per_group
    return (channel >= low) & (channel < low + per_group) & (lane >= 0) & (lane < GROUPS)


def spread(xs_ref, f, e, v):
    left, right = roll_both(v.astype(F32), 1)
    xs_ref[f, e, 0:16] = left.astype(BF16)
    xs_ref[f, e, 16:32] = v
    xs_ref[f, e, 32:48] = right.astype(BF16)


def frame_weights(w_ref, flags_ref):
    taps = w_ref.shape[1] - 8
    whole = w_ref[:, :taps]
    lane = lax.broadcasted_iota(jnp.int32, (1, taps), 1)
    result = []
    for j in range(4):
        u0 = flags_ref[2 * j : 2 * j + 1, 0:1]
        u1 = flags_ref[2 * j + 1 : 2 * j + 2, 0:1]
        keep = jnp.where(lane < taps // 3, u0, jnp.where(lane < 2 * taps // 3, u1, 1.0)).astype(BF16)
        result.append(whole * keep)
    bias = w_ref[:, taps:].astype(F32)
    return result, bias[:, 0:1] + bias[:, 1:2] + bias[:, 2:3]


def hidden_t(weights, bias, xs_ref, j, r):
    patches = jnp.concatenate([xs_ref[j + k, r : r + 3].reshape(144, LANES) for k in range(3)], axis=0)
    return jnp.dot(weights, patches, preferred_element_type=F32) + bias


def sums_kernel(width, tiles, flags_ref, above_ref, picked_ref, w_ref, sums_ref, xs_ref, s1_ref, s2_ref):
    channels = w_ref.shape[0]
    tile = lax.axis_index("tile")
    for f in range(6):
        for e in range(4):
            spread(xs_ref, f, e, (above_ref, picked_ref)[e // 2][f, e % 2])
        xs_ref[f, 4] = jnp.zeros((48, LANES), BF16)
    weights, bias = frame_weights(w_ref, flags_ref)
    rest = lax.broadcasted_iota(jnp.int32, (channels, 128), 1) < width - 128

    def row(j, r):
        h = hidden_t(weights[j], bias, xs_ref, j, r).astype(BF16).astype(F32)
        a, b = h[:, :128], jnp.where(rest, h[:, 128:], 0.0)
        if r == 0:
            a, b = jnp.where(tile > 0, a, 0.0), jnp.where(tile > 0, b, 0.0)
        return a + b, a * a + b * b

    for j in range(4):
        a1, a2 = row(j, 0)
        b1, b2 = row(j, 1)
        s1_ref[j] = a1 + b1
        s2_ref[j] = a2 + b2

    @pl.when(tile == tiles - 1)
    def _():
        for j in range(4):
            c1, c2 = row(j, 2)
            s1_ref[j] = s1_ref[j] + c1
            s2_ref[j] = s2_ref[j] + c2

    d1 = jnp.zeros((channels, 128), F32)
    d2 = jnp.zeros((channels, 128), F32)
    for j in range(4):
        mask = group_mask(channels, j)
        d1 = jnp.where(mask, jnp.sum(s1_ref[j], axis=1, keepdims=True), d1)
        d2 = jnp.where(mask, jnp.sum(s2_ref[j], axis=1, keepdims=True), d2)
    block = jnp.concatenate([jnp.sum(d1, axis=0, keepdims=True), jnp.sum(d2, axis=0, keepdims=True)], axis=0)
    sums_ref[...] = jnp.broadcast_to(block[None], sums_ref.shape)


def hidden_kernel(
    width, flags_ref, above_ref, picked_ref, below_ref, w_ref, w_mid_hbm, hidden_ref, early_ref, xs_ref, sem
):
    fetch = pltpu.make_async_copy(w_mid_hbm.at[0:EARLY], early_ref, sem)
    fetch.start()
    for f in range(6):
        for e in range(6):
            spread(xs_ref, f, e, (above_ref, picked_ref, below_ref)[e // 2][f, e % 2])
    weights, bias = frame_weights(w_ref, flags_ref)
    for j in range(4):
        for r in range(4):
            hidden_ref[j, r] = hidden_t(weights[j], bias, xs_ref, j, r).T[:width].astype(BF16)
    fetch.wait()


def decode_kernel(
    entries, tiles, flags_ref, sums_ref, h_ref, early_ref, w_hbm, gain_ref, bias_ref, out_hbm, act_ref, acc_ref, late_ref, out_ref, sem, out_sem
):
    late = pltpu.make_async_copy(w_hbm.at[EARLY:27], late_ref, sem)
    late.start()
    width, channels = h_ref.shape[2:]
    per_group = channels // GROUPS
    tile = lax.axis_index("tile")
    total = jnp.sum(sums_ref[...], axis=0)
    average = total[0:1] / entries
    variance = total[1:2] / entries - average * average
    rstd = lax.rsqrt(variance + 1e-06)
    packed = jnp.concatenate(split3(average) + split3(rstd) + [jnp.zeros((2, 128), F32)], axis=0).astype(BF16)
    source = lax.broadcasted_iota(jnp.int32, (128, LANES), 0)
    channel = lax.broadcasted_iota(jnp.int32, (128, LANES), 1)
    position = lax.broadcasted_iota(jnp.int32, (width, channels), 0)
    half_gain = 0.5 * gain_ref[...]
    results = []
    bias = bias_ref[...]

    def activate(j):
        start = per_group * (source - GROUPS * j)
        expand = (channel >= start) & (channel < start + per_group) & (source >= GROUPS * j) & (source < GROUPS * (j + 1))
        wide = jnp.dot(packed, jnp.where(expand, 1.0, 0.0).astype(BF16), preferred_element_type=F32)
        mean = (wide[0:1] + wide[1:2] + wide[2:3])[:, :channels]
        scale = (wide[3:4] + wide[4:5] + wide[5:6])[:, :channels] * half_gain
        for r in range(4):
            u = (h_ref[j, r].astype(F32) - mean) * scale
            a = u + u * jnp.tanh(u)
            if r == 0:
                a = jnp.where(tile > 0, a, 0.0)
            if r == 3:
                a = jnp.where(tile < tiles - 1, a, 0.0)
            left, right = roll_both(a, 0)
            act_ref[j, r, 0] = jnp.where(position > 0, left, 0.0).astype(BF16)
            act_ref[j, r, 1] = a.astype(BF16)
            act_ref[j, r, 2] = jnp.where(position < width - 1, right, 0.0).astype(BF16)

    def convolve(i, k):
        taps = [early_ref[t] if t < EARLY else late_ref[t - EARLY] for t in range(9 * k, 9 * k + 9)]
        for r in range(2):
            term = None
            for dy in range(3):
                for dx in range(3):
                    d = jnp.dot(act_ref[i + k, r + dy, dx], taps[3 * dy + dx], preferred_element_type=F32)
                    term = d if term is None else term + d
            if k < 2:
                flag = flags_ref[2 * (i + 2) + k : 2 * (i + 2) + k + 1, :channels]
                term = jnp.where(flag > 0.0, term, 0.0)
            if k == 0:
                acc_ref[i, r] = term
            elif k == 1:
                acc_ref[i, r] = acc_ref[i, r] + term
            else:
                y = acc_ref[i, r] + term + bias + h_ref[2 + i, r + 1].astype(F32)
                out_ref[i, r] = y.astype(BF16)
                results.append(pltpu.make_async_copy(out_ref.at[i, r], out_hbm.at[i, r], out_sem.at[i, r]))
                results[-1].start()

    activate(0)
    convolve(0, 0)
    activate(1)
    convolve(1, 0)
    activate(2)
    late.wait()
    convolve(0, 1)
    convolve(1, 1)
    activate(3)
    convolve(0, 2)
    convolve(1, 2)
    for copy in results:
        copy.wait()


def body(latents, frame_slot, lengths, w_in, bias_in, norm_gain, w_mid, bias_mid):
    rows = latents.shape[1]
    zc = w_in.shape[0]
    channels = w_in.shape[2]
    width = latents.shape[2] // zc
    tiles = lax.axis_size("tile")
    whole = jnp.concatenate([frame_slot, lengths])
    cores = [[2 * y + c for y in CHIPS] for c in range(2)]
    column = lax.all_to_all(jnp.broadcast_to(latents[None], (8,) + latents.shape), "tm", 0, 0, axis_index_groups=cores)
    gathered = lax.all_gather(column, "tm", axis=0, axis_index_groups=[[2 * y, 2 * y + 1] for y in range(8)])
    gathered = gathered.reshape((32,) + latents.shape[1:])

    def pick_body(*refs):
        pick_kernel(zc, frame_slot.shape[0], *refs)

    picked, flags = pl.pallas_call(
        pick_body,
        out_shape=[jax.ShapeDtypeStruct((6, rows, zc, LANES), BF16), jax.ShapeDtypeStruct((8, LANES), F32)],
        in_specs=[SMEM, VMEM],
        out_specs=[VMEM, VMEM],
        scratch_shapes=[
            pltpu.SMEM(frame_slot.shape, jnp.int32),
            pltpu.VMEM((6,) + latents.shape[1:], F32),
        ],
        compiler_params=PARAMS,
        name="pick",
    )(whole, gathered)
    above = lax.ppermute(picked, "tile", [(i, i + 1) for i in range(tiles - 1)])
    below = lax.ppermute(picked, "tile", [(i + 1, i) for i in range(tiles - 1)])
    w_in = jnp.transpose(w_in, (1, 0, 2)).reshape(27 * zc, channels)
    high = lax.reduce_precision(bias_in, 8, 7)
    middle = lax.reduce_precision(bias_in - high, 8, 7)
    parts = jnp.stack([high, middle, bias_in - high - middle] + [jnp.zeros_like(bias_in)] * 5)
    w_in = jnp.concatenate([w_in, parts.astype(BF16)], axis=0).T
    w_mid = jnp.transpose(w_mid, (1, 0, 2))

    def sums_body(*refs):
        sums_kernel(width, tiles, *refs)

    def hidden_body(*refs):
        hidden_kernel(width, *refs)

    sums = pl.pallas_call(
        sums_body,
        out_shape=jax.ShapeDtypeStruct((tiles, 2, 128), F32),
        in_specs=[VMEM] * 4,
        out_specs=VMEM,
        scratch_shapes=[
            pltpu.VMEM((6, 5, 3 * zc, LANES), BF16),
            pltpu.VMEM((4, channels, 128), F32),
            pltpu.VMEM((4, channels, 128), F32),
        ],
        compiler_params=PARAMS,
        name="sums",
    )(flags, above, picked, w_in)
    sums = lax.all_to_all(sums, "tile", 0, 0, axis_index_groups=[TILES])
    hidden, early = pl.pallas_call(
        hidden_body,
        out_shape=[
            jax.ShapeDtypeStruct((4, 4, width, channels), BF16),
            jax.ShapeDtypeStruct((EARLY, channels, channels), BF16),
        ],
        in_specs=[VMEM] * 5 + [HBM],
        out_specs=[VMEM, VMEM],
        scratch_shapes=[
            pltpu.VMEM((6, 6, 3 * zc, LANES), BF16),
            pltpu.SemaphoreType.DMA,
        ],
        compiler_params=pltpu.CompilerParams(vmem_limit_bytes=50000 * 1024),
        cost_estimate=pl.CostEstimate(flops=4_000_000_000, bytes_accessed=2_000_000, transcendentals=0),
        name="hidden",
    )(flags, above, picked, below, w_in, w_mid)
    entries = float(rows * tiles * width * (channels // GROUPS))

    def decode_body(*refs):
        decode_kernel(entries, tiles, *refs)

    return pl.pallas_call(
        decode_body,
        out_shape=jax.ShapeDtypeStruct((2, rows, width, channels), BF16),
        in_specs=[VMEM, VMEM, VMEM, VMEM, HBM, VMEM, VMEM],
        out_specs=HBM,
        scratch_shapes=[
            pltpu.VMEM((4, 4, 3, width, channels), BF16),
            pltpu.VMEM((2, 2, width, channels), F32),
            pltpu.VMEM((27 - EARLY, channels, channels), BF16),
            pltpu.VMEM((2, 2, width, channels), BF16),
            pltpu.SemaphoreType.DMA,
            pltpu.SemaphoreType.DMA((2, 2)),
        ],
        compiler_params=pltpu.CompilerParams(vmem_limit_bytes=52000 * 1024),
        name="decode",
    )(flags, sums, hidden, early, w_mid, norm_gain[None, :], bias_mid[None, :])


def solution(mesh):
    return jax.shard_map(
        body,
        mesh=mesh,
        in_specs=(P("tm", "tile", None), P(), P(), P(), P(), P(), P(), P()),
        out_specs=P("tm", "tile", None, None),
        check_vma=False,
    )
```
